32 devices in a mesh: freq: 8 (over z, y), inp: 4 (over x, core).
Axes of the slice: x: 2, y: 2, z: 4, core: 2. Of those that a mesh axis runs over, the one named last changes fastest.
Arguments:
- voltages: int32 [24, 2048, 1024], P('freq', None, 'inp'), may hold values from -128 to 127
- taps: float32 [12, 2048], replicated, may hold values from -0.013671875 to 0.013671875
- start: int32 [8, 2, 1024], replicated, may hold values from -127 to 127
Outputs:
- cleaned: bfloat16 [1024, 24, 2, 1024], P('freq', None, None, 'inp')
- ritz_matrix: float32 [1024, 8, 8], P('freq')
The draws below stay inside these ranges and needn't reach their ends.
Inputs may be any that keep to these rules, and one draw needn't show every extreme that they name: `voltages`: 8-bit voltage samples.
All inputs are finite; a program needn't handle non-finite values.
Results may differ from the reference program's by a relative error of at most 0.0052.
Values may be sent and summed in bfloat16 or wider, within the bound.
A program may use at most 192 MiB of HBM per device.

```python
import math
import jax
import jax.numpy as jnp
from jax import lax

NFFT = 2048
NCH = 1024
NIN = 1024
TAPS = 12
BLOCK = 8
ITERS = 4
SPECTRA = 24


def with_ends(drawn, own_key, least, high):
    longest = drawn.shape.index(max(drawn.shape))
    spots = []
    for shift in (0, 1):
        where = [jax.random.randint(jax.random.fold_in(own_key, axis), (), 0, length) for axis, length in enumerate(drawn.shape)]
        where[longest] = (where[longest] + shift) % drawn.shape[longest]
        spots.append(tuple(where))
    return drawn.at[spots[0]].set(least).at[spots[1]].set(high)


def centred(rng, extent, scale, limit, held_as=jnp.bfloat16):
    result = scale * jax.random.normal(rng, extent, jnp.float32)
    return jnp.clip(result, min=-limit, max=limit).astype(held_as)


def setup_inputs(seed: int = 0) -> dict:
    keys = jax.random.split(jax.random.key(seed), 4)
    return {
        "voltages": with_ends(jax.random.randint(keys[0], (SPECTRA, NFFT, NIN), -128, 128), jax.random.fold_in(keys[0], 1), -128, 127).astype(jnp.int32),
        "taps": centred(keys[1], (TAPS, NFFT), (TAPS * 16384) ** -0.5, 0.013671875, jnp.float32),
        "start": with_ends(jax.random.randint(keys[2], (BLOCK, 2, NIN), -127, 128), jax.random.fold_in(keys[2], 1), -127, 127).astype(jnp.int32),
    }


def channelize(volt_block, taps):
    frames = volt_block.astype(jnp.float32)
    filtered = jnp.zeros(frames.shape, jnp.float32)
    for tap_index in range(TAPS):
        filtered = filtered + taps[tap_index][None, :, None] * jnp.roll(frames, TAPS - 1 - tap_index, axis=0)
    spectrum = jnp.fft.rfft(filtered, axis=1)[:, :NCH, :] / math.sqrt(NCH)
    paired = jnp.stack([jnp.real(spectrum), jnp.imag(spectrum)], axis=2)
    return jnp.transpose(paired, (1, 0, 2, 3)).astype(jnp.bfloat16)

def clean_channel(spectrum, start_rows):
    highest = lax.Precision.HIGHEST
    channel_data = spectrum.reshape(SPECTRA, 2 * NIN).astype(jnp.float32)
    basis_rows = start_rows
    for iteration in range(ITERS):
        projected = jnp.dot(basis_rows, channel_data.T, precision=highest)
        mapped = jnp.dot(projected, channel_data, precision=highest) / SPECTRA
        gram_matrix = jnp.dot(mapped, mapped.T, precision=highest)
        lower_factor = jnp.linalg.cholesky(gram_matrix)
        basis_rows = lax.linalg.triangular_solve(lower_factor, mapped, left_side=True, lower=True)
    projected = jnp.dot(basis_rows, channel_data.T, precision=highest)
    ritz_matrix = jnp.dot(projected, projected.T, precision=highest) / SPECTRA
    cleaned = channel_data - jnp.dot(projected.T, basis_rows, precision=highest)
    return (cleaned.reshape(SPECTRA, 2, NIN).astype(jnp.bfloat16), ritz_matrix)

def reference(voltages, taps, start):
    block_len = min(NIN, 128)
    block_count = NIN // block_len
    volt_blocks = jnp.transpose(voltages.reshape(SPECTRA, NFFT, block_count, block_len), (2, 0, 1, 3))
    spectra = lax.map(lambda volt_block: channelize(volt_block, taps), volt_blocks)
    spectra = jnp.transpose(spectra, (1, 2, 3, 0, 4)).reshape(NCH, SPECTRA, 2, NIN)
    start_rows = start.reshape(BLOCK, 2 * NIN).astype(jnp.float32)
    cleaned, ritz_matrix = lax.map(lambda spectrum: clean_channel(spectrum, start_rows), spectra)
    return (cleaned, ritz_matrix)
```

```python
import functools
import math

import jax
import jax.numpy as jnp
import ml_dtypes
import numpy as np
from jax import lax
from jax.experimental import pallas as pl
from jax.experimental.pallas import tpu as pltpu
from jax.sharding import PartitionSpec as P

ITERS = 4
CHUNKS = 2
LANES = 128
MESH = pl.DeviceIdType.MESH


def dft_tables(frame_len, group_count):
    half = frame_len // 2
    pairs = half // 2
    sample = np.arange(half, dtype=np.int64)[:, None]
    tables = []
    for parity in (0, 1):
        channel = 2 * np.arange(pairs, dtype=np.int64)[None, :] + parity
        angle = 2.0 * np.pi * ((sample * channel) % frame_len) / frame_len
        scale = 1.0 / math.sqrt(half)
        real = (np.cos(angle) * scale).reshape(half, group_count, 1, pairs // group_count)
        imag = (-np.sin(angle) * scale).reshape(half, group_count, 1, pairs // group_count)
        table = np.concatenate([real, imag], axis=2).reshape(half, half)
        high = table.astype(ml_dtypes.bfloat16)
        low = (table - high.astype(np.float64)).astype(ml_dtypes.bfloat16)
        tables += [high, low]
    return np.stack(tables)


def channelize_kernel(
    count, slots, tap_count, volts_ref, taps_ref, table_hbm, turned_ref,
    gathered, table, halves, outgoing, table_sem, send_a, recv_a, send_b, recv_b,
):
    me = lax.axis_index("freq")
    frames = count * slots
    half = table.shape[1]
    rows = volts_ref.shape[3]

    table_copy = pltpu.make_async_copy(table_hbm, table, table_sem)
    table_copy.start()
    barrier = pltpu.get_barrier_semaphore()
    for step in range(1, count):
        peer = lax.rem(me + step, count)
        pl.semaphore_signal(barrier, inc=1, device_id={"freq": peer}, device_id_type=MESH)
    pl.semaphore_wait(barrier, count - 1)

    def voltage_copy(chunk, step):
        peer = lax.rem(me + step, count)
        return pltpu.make_async_remote_copy(
            src_ref=volts_ref.at[peer, chunk],
            dst_ref=gathered.at[chunk, me],
            send_sem=send_a.at[chunk, step - 1],
            recv_sem=recv_a.at[chunk, step - 1],
            device_id={"freq": peer},
            device_id_type=MESH,
        )

    def spectra_copy(chunk, step):
        peer = lax.rem(me + step, count)
        return pltpu.make_async_remote_copy(
            src_ref=outgoing.at[peer, chunk],
            dst_ref=turned_ref.at[me, chunk],
            send_sem=send_b.at[chunk, step - 1],
            recv_sem=recv_b.at[chunk, step - 1],
            device_id={"freq": peer},
            device_id_type=MESH,
        )

    order = sorted(range(1, count), key=lambda step: -min(step, count - step))
    first = [voltage_copy(0, step) for step in order]
    for copy in first:
        copy.start()
    for chunk in range(CHUNKS):
        gathered[chunk, me] = volts_ref[me, chunk]
    arriving = first
    for chunk in range(CHUNKS):
        for copy in arriving:
            copy.wait_send()
        following = []
        if chunk + 1 < CHUNKS:
            following = [voltage_copy(chunk + 1, step) for step in order]
            for copy in following:
                copy.start()
        for copy in arriving:
            copy.wait_recv()
        arriving = following

        def filter_tile(tile, carry):
            sums = []
            for part in (0, 1):
                at = pl.ds(pl.multiple_of(tile * LANES + part * half, LANES), LANES)
                window = gathered[chunk, :, :, :, at].astype(jnp.float32)
                window = window.reshape(frames, rows, LANES)
                extended = jnp.concatenate([window[frames - tap_count + 1 :], window], axis=0)
                total = taps_ref[0:1, at][None] * extended[:frames]
                for tap in range(1, tap_count):
                    total = total + taps_ref[tap : tap + 1, at][None] * extended[tap : tap + frames]
                sums.append(total.reshape(frames * rows, LANES))
            at = pl.ds(pl.multiple_of(tile * LANES, LANES), LANES)
            for index, value in ((0, sums[0] + sums[1]), (2, sums[0] - sums[1])):
                high = value.astype(jnp.bfloat16)
                halves[index, :, at] = high
                halves[index + 1, :, at] = (value - high.astype(jnp.float32)).astype(jnp.bfloat16)
            return carry

        lax.fori_loop(0, half // LANES, filter_tile, 0)
        if chunk == 0:
            table_copy.wait()

        def transform_tile(pair, carry):
            at = pl.ds(pl.multiple_of(pair * 2 * LANES, 2 * LANES), 2 * LANES)
            for parity in (0, 1):
                high, low = halves[2 * parity], halves[2 * parity + 1]
                table_high = table[2 * parity, :, at]
                table_low = table[2 * parity + 1, :, at]
                dot = functools.partial(jnp.dot, preferred_element_type=jnp.float32)
                result = dot(low, table_high) + dot(high, table_low) + dot(high, table_high)
                result = result.astype(jnp.bfloat16)
                outgoing[2 * pair, chunk, parity] = result[:, :LANES]
                outgoing[2 * pair + 1, chunk, parity] = result[:, LANES:]
            return carry

        lax.fori_loop(0, count // 2, transform_tile, 0)
        for step in order:
            spectra_copy(chunk, step).start()
        turned_ref[me, chunk] = outgoing[me, chunk]
    for chunk in range(CHUNKS):
        for step in order:
            spectra_copy(chunk, step).wait()


def channelize(voltages, taps):
    slots, frame_len, inputs_local = voltages.shape
    count = lax.axis_size("freq")
    half = frame_len // 2
    rows = inputs_local // (count * CHUNKS)
    volts = voltages.astype(jnp.bfloat16).reshape(slots, frame_len, count, CHUNKS, rows)
    volts = jnp.transpose(volts, (2, 3, 0, 4, 1))
    table = jnp.asarray(dft_tables(frame_len, count))
    all_rows = count * slots * rows
    vmem = pl.BlockSpec(memory_space=pltpu.VMEM)
    turned = pl.pallas_call(
        functools.partial(channelize_kernel, count, slots, taps.shape[0]),
        out_shape=jax.ShapeDtypeStruct((count, CHUNKS, 2, all_rows, LANES), jnp.bfloat16),
        in_specs=[vmem, vmem, pl.BlockSpec(memory_space=pl.ANY)],
        out_specs=vmem,
        scratch_shapes=[
            pltpu.VMEM((CHUNKS, count, slots, rows, frame_len), jnp.bfloat16),
            pltpu.VMEM((4, half, half), jnp.bfloat16),
            pltpu.VMEM((4, all_rows, half), jnp.bfloat16),
            pltpu.VMEM((count, CHUNKS, 2, all_rows, LANES), jnp.bfloat16),
            pltpu.SemaphoreType.DMA,
            pltpu.SemaphoreType.DMA((CHUNKS, count - 1)),
            pltpu.SemaphoreType.DMA((CHUNKS, count - 1)),
            pltpu.SemaphoreType.DMA((CHUNKS, count - 1)),
            pltpu.SemaphoreType.DMA((CHUNKS, count - 1)),
        ],
        compiler_params=pltpu.CompilerParams(
            collective_id=0, has_side_effects=True, vmem_limit_bytes=48 * 1024 * 1024
        ),
        name="channelize",
    )(volts, taps, table)
    turned = turned.reshape(count, CHUNKS, 2, count * slots, rows, 2, LANES // 2)
    turned = jnp.transpose(turned, (6, 2, 3, 5, 0, 1, 4))
    return turned.reshape(LANES, count * slots, 2, inputs_local)


def subspace_kernel(gram_ref, keep_ref, ritz_ref):
    block = ritz_ref.shape[0]
    frames = keep_ref.shape[0]

    def times_gram(left):
        total = left[:, 0:1] * gram_ref[block][None]
        for frame in range(1, frames):
            total = total + left[:, frame : frame + 1] * gram_ref[block + frame][None]
        return total

    projected = gram_ref[:block]
    coefficients = None
    for iteration in range(ITERS):
        mapped = projected * (1.0 / frames)
        spread = times_gram(mapped)
        columns = [jnp.sum(spread * mapped[k][None], axis=1) for k in range(block)]
        remaining = [mapped[k] for k in range(block)]
        for k in range(block):
            inverse = lax.rsqrt(columns[k][k : k + 1])
            inverse = inverse * (1.5 - 0.5 * columns[k][k : k + 1] * inverse * inverse)
            factor = columns[k] * inverse
            remaining[k] = remaining[k] * inverse
            for j in range(k + 1, block):
                remaining[j] = remaining[j] - factor[j : j + 1] * remaining[k]
                columns[j] = columns[j] - factor[j : j + 1] * factor
        coefficients = jnp.stack(remaining)
        projected = times_gram(coefficients)
    for k in range(block):
        ritz_ref[k] = jnp.sum(projected * projected[k][None], axis=1) * (1.0 / frames)
    row = lax.broadcasted_iota(jnp.int32, keep_ref.shape[1:], 0)
    for frame in range(frames):
        removed = projected[0][frame : frame + 1] * coefficients[0]
        for k in range(1, block):
            removed = removed + projected[k][frame : frame + 1] * coefficients[k]
        keep_ref[frame] = jnp.where(row == frame, 1.0, 0.0) - removed


def clean(turned, start_local):
    channels, frames, parts, inputs_local = turned.shape
    block = start_local.shape[0]
    data = turned.reshape(channels, frames, parts * inputs_local)
    begin = start_local.reshape(block, parts * inputs_local).astype(jnp.bfloat16)
    stacked = jnp.concatenate(
        [jnp.broadcast_to(begin[None], (channels,) + begin.shape), data], axis=1
    )
    gram = jnp.einsum("czr,cmr->czm", stacked, data, preferred_element_type=jnp.float32)
    gram = jnp.transpose(lax.psum(gram, "inp"), (1, 2, 0))
    keep, ritz = pl.pallas_call(
        subspace_kernel,
        out_shape=(
            jax.ShapeDtypeStruct((frames, frames, channels), jnp.float32),
            jax.ShapeDtypeStruct((block, block, channels), jnp.float32),
        ),
        compiler_params=pltpu.CompilerParams(vmem_limit_bytes=32 * 1024 * 1024),
        name="subspace",
    )(gram)
    keep = jnp.transpose(keep, (2, 0, 1))
    cleaned = jnp.einsum(
        "cmn,cnr->cmr", keep, data.astype(jnp.float32), precision=lax.Precision.HIGHEST
    )
    cleaned = cleaned.astype(jnp.bfloat16).reshape(turned.shape)
    return cleaned, jnp.transpose(ritz, (2, 0, 1))


def from_behind(value, axis, steps):
    count = lax.axis_size(axis)
    pairs = [(source, (source + steps) % count) for source in range(count)]
    return lax.ppermute(value, axis, pairs)


def project_rows(basis_rows, channel_data):
    projected = jnp.einsum(
        "ckr,cmr->ckm", basis_rows, channel_data, precision=lax.Precision.HIGHEST
    )
    return lax.psum(projected, "inp")


def subspace_clean(turned, start_block):
    highest = lax.Precision.HIGHEST
    channel_local, spectra_count, part_count, inputs_width = turned.shape
    row_count = part_count * inputs_width
    channel_data = turned.reshape(channel_local, spectra_count, row_count).astype(jnp.float32)
    start_rows = start_block.reshape(start_block.shape[0], row_count).astype(jnp.float32)
    basis_rows = jnp.broadcast_to(start_rows[None], (channel_local,) + start_rows.shape)
    for iteration in range(ITERS):
        projected = project_rows(basis_rows, channel_data)
        mapped = (
            jnp.einsum("ckm,cmr->ckr", projected, channel_data, precision=highest) / spectra_count
        )
        gram_matrix = jnp.einsum("ckr,cjr->ckj", mapped, mapped, precision=highest)
        gram_matrix = lax.psum(gram_matrix, "inp")
        lower_factor = jnp.linalg.cholesky(gram_matrix)
        basis_rows = lax.linalg.triangular_solve(lower_factor, mapped, left_side=True, lower=True)
    projected = project_rows(basis_rows, channel_data)
    ritz_matrix = (
        jnp.einsum("ckm,cjm->ckj", projected, projected, precision=highest) / spectra_count
    )
    cleaned = channel_data - jnp.einsum("ckm,ckr->cmr", projected, basis_rows, precision=highest)
    cleaned = cleaned.reshape(channel_local, spectra_count, part_count, inputs_width).astype(
        jnp.bfloat16
    )
    return (cleaned, ritz_matrix)


def general_shards(voltages, taps, start):
    slot_count = voltages.shape[0]
    frame_len = voltages.shape[1]
    inputs_local = voltages.shape[2]
    channel_count = frame_len // 2
    tap_count = taps.shape[0]
    frame_stack = voltages.astype(jnp.bfloat16)
    history_len = tap_count - 1
    group_count = lax.axis_size("freq")
    portions = [frame_stack]
    shift_count = (history_len - 1) // slot_count + 1
    for distance in range(1, shift_count + 1):
        first_frame = max(0, distance * slot_count - history_len)
        portion = frame_stack[first_frame:]
        offset_mod = distance % group_count
        arrived = from_behind(portion, "freq", offset_mod)
        portions = [arrived] + portions
    extended = jnp.concatenate(portions, axis=0)
    filtered = jnp.zeros((slot_count, frame_len, inputs_local), jnp.float32)
    for tap_index in range(tap_count):
        window = extended[tap_index : tap_index + slot_count].astype(jnp.float32)
        filtered = filtered + taps[tap_index][None, :, None] * window
    channel_idx = lax.broadcasted_iota(jnp.int32, (channel_count, frame_len), 0)
    sample_idx = lax.broadcasted_iota(jnp.int32, (channel_count, frame_len), 1)
    angles = (channel_idx * sample_idx % frame_len).astype(jnp.float32) * (
        2.0 * math.pi / frame_len
    )
    dft_scale = 1.0 / math.sqrt(channel_count)
    cosine = jnp.cos(angles)
    sine_table = jnp.sin(angles)
    real_part = (
        jnp.einsum("kn,sni->ksi", cosine, filtered, precision=lax.Precision.HIGHEST) * dft_scale
    )
    imag_part = (
        -jnp.einsum("kn,sni->ksi", sine_table, filtered, precision=lax.Precision.HIGHEST)
        * dft_scale
    )
    spectra = jnp.stack([real_part, imag_part], axis=2).astype(jnp.bfloat16)
    turned = lax.all_to_all(spectra, "freq", split_axis=0, concat_axis=1, tiled=True)
    start_local = lax.dynamic_slice_in_dim(
        start, lax.axis_index("inp") * inputs_local, inputs_local, 2
    )
    cleaned, ritz_matrix = subspace_clean(turned, start_local)
    return (cleaned, ritz_matrix)


def start_columns(start, inputs_local):
    return lax.dynamic_slice_in_dim(start, lax.axis_index("inp") * inputs_local, inputs_local, 2)


def shards(voltages, taps, start):
    slots, frame_len, inputs_local = voltages.shape
    count = lax.axis_size("freq")
    fits = (
        count % 2 == 0
        and frame_len // 2 == count * LANES
        and inputs_local % (count * CHUNKS * 16) == 0
        and count * slots <= 32
        and taps.shape[0] <= count * slots
    )
    if not fits:
        return general_shards(voltages, taps, start)
    return clean(channelize(voltages, taps), start_columns(start, inputs_local))


def solution(mesh):
    placed = (P("freq", None, "inp"), P(), P())
    return jax.shard_map(
        shards,
        mesh=mesh,
        in_specs=placed,
        out_specs=(P("freq", None, None, "inp"), P("freq", None, None)),
        check_vma=False,
    )
```

```python
import functools
import math

import jax
import jax.numpy as jnp
import ml_dtypes
import numpy as np
from jax import lax
from jax.experimental import pallas as pl
from jax.experimental.pallas import tpu as pltpu
from jax.sharding import PartitionSpec as P

ITERS = 4
CHUNKS = 2
LANES = 128
MESH = pl.DeviceIdType.MESH


def dft_tables(frame_len, group_count):
    half = frame_len // 2
    pairs = half // 2
    sample = np.arange(half, dtype=np.int64)[:, None]
    tables = []
    for parity in (0, 1):
        channel = 2 * np.arange(pairs, dtype=np.int64)[None, :] + parity
        angle = 2.0 * np.pi * ((sample * channel) % frame_len) / frame_len
        scale = 1.0 / math.sqrt(half)
        real = (np.cos(angle) * scale).reshape(half, group_count, 1, pairs // group_count)
        imag = (-np.sin(angle) * scale).reshape(half, group_count, 1, pairs // group_count)
        table = np.concatenate([real, imag], axis=2).reshape(half, half)
        high = table.astype(ml_dtypes.bfloat16)
        low = (table - high.astype(np.float64)).astype(ml_dtypes.bfloat16)
        tables += [high, low]
    return np.stack(tables)


def channelize_kernel(
    count, slots, tap_count, volts_ref, taps_ref, table_hbm, spectra_ref,
    gathered, table, halves, outgoing, landed, table_sem, send_a, recv_a, send_b, recv_b,
):
    me = lax.axis_index("freq")
    frames = count * slots
    half = table.shape[1]
    rows = volts_ref.shape[3]

    table_copy = pltpu.make_async_copy(table_hbm, table, table_sem)
    table_copy.start()
    barrier = pltpu.get_barrier_semaphore()
    for step in range(1, count):
        peer = lax.rem(me + step, count)
        pl.semaphore_signal(barrier, inc=1, device_id={"freq": peer}, device_id_type=MESH)
    pl.semaphore_wait(barrier, count - 1)

    def voltage_copy(chunk, step):
        peer = lax.rem(me + step, count)
        return pltpu.make_async_remote_copy(
            src_ref=volts_ref.at[peer, chunk],
            dst_ref=gathered.at[chunk, me],
            send_sem=send_a.at[chunk, step - 1],
            recv_sem=recv_a.at[chunk, step - 1],
            device_id={"freq": peer},
            device_id_type=MESH,
        )

    def spectra_copy(chunk, step):
        peer = lax.rem(me + step, count)
        return pltpu.make_async_remote_copy(
            src_ref=outgoing.at[peer, chunk],
            dst_ref=landed.at[me, chunk],
            send_sem=send_b.at[chunk, step - 1],
            recv_sem=recv_b.at[chunk, step - 1],
            device_id={"freq": peer},
            device_id_type=MESH,
        )

    order = sorted(range(1, count), key=lambda step: -min(step, count - step))
    first = [voltage_copy(0, step) for step in order]
    for copy in first:
        copy.start()
    for chunk in range(CHUNKS):
        gathered[chunk, me] = volts_ref[me, chunk]
    arriving = first
    for chunk in range(CHUNKS):
        for copy in arriving:
            copy.wait_send()
        following = []
        if chunk + 1 < CHUNKS:
            following = [voltage_copy(chunk + 1, step) for step in order]
            for copy in following:
                copy.start()
        for copy in arriving:
            copy.wait_recv()
        arriving = following

        def filter_tile(tile, carry):
            sums = []
            for part in (0, 1):
                at = pl.ds(pl.multiple_of(tile * LANES + part * half, LANES), LANES)
                window = gathered[chunk, :, :, :, at].astype(jnp.float32)
                window = window.reshape(frames, rows, LANES)
                extended = jnp.concatenate([window[frames - tap_count + 1 :], window], axis=0)
                total = taps_ref[0:1, at][None] * extended[:frames]
                for tap in range(1, tap_count):
                    total = total + taps_ref[tap : tap + 1, at][None] * extended[tap : tap + frames]
                sums.append(total.reshape(frames * rows, LANES))
            at = pl.ds(pl.multiple_of(tile * LANES, LANES), LANES)
            for index, value in ((0, sums[0] + sums[1]), (2, sums[0] - sums[1])):
                high = value.astype(jnp.bfloat16)
                halves[index, :, at] = high
                halves[index + 1, :, at] = (value - high.astype(jnp.float32)).astype(jnp.bfloat16)
            return carry

        lax.fori_loop(0, half // LANES, filter_tile, 0)
        if chunk == 0:
            table_copy.wait()

        def transform_tile(pair, carry):
            at = pl.ds(pl.multiple_of(pair * 2 * LANES, 2 * LANES), 2 * LANES)
            for parity in (0, 1):
                high, low = halves[2 * parity], halves[2 * parity + 1]
                table_high = table[2 * parity, :, at]
                table_low = table[2 * parity + 1, :, at]
                dot = functools.partial(jnp.dot, preferred_element_type=jnp.float32)
                result = dot(low, table_high) + dot(high, table_low) + dot(high, table_high)
                result = result.astype(jnp.bfloat16)
                outgoing[2 * pair, chunk, parity] = result[:, :LANES]
                outgoing[2 * pair + 1, chunk, parity] = result[:, LANES:]
            return carry

        lax.fori_loop(0, count // 2, transform_tile, 0)
        for step in order:
            spectra_copy(chunk, step).start()
        landed[me, chunk] = outgoing[me, chunk]
    for chunk in range(CHUNKS):
        for step in order:
            spectra_copy(chunk, step).wait()

        def turn_frame(index, carry):
            parity, frame = lax.div(index, frames), lax.rem(index, frames)
            at = pl.ds(pl.multiple_of(frame * rows, rows), rows)
            block = landed[:, chunk, parity, at, :].reshape(count * rows, LANES)
            spectra_ref[parity, frame, :, chunk * LANES : (chunk + 1) * LANES] = block.T
            return carry

        lax.fori_loop(0, 2 * frames, turn_frame, 0)


def channelize(voltages, taps):
    slots, frame_len, inputs_local = voltages.shape
    count = lax.axis_size("freq")
    half = frame_len // 2
    rows = inputs_local // (count * CHUNKS)
    volts = voltages.astype(jnp.bfloat16).reshape(slots, frame_len, CHUNKS, count, rows)
    volts = jnp.transpose(volts, (3, 2, 0, 4, 1))
    table = jnp.asarray(dft_tables(frame_len, count))
    all_rows = count * slots * rows
    vmem = pl.BlockSpec(memory_space=pltpu.VMEM)
    spectra = pl.pallas_call(
        functools.partial(channelize_kernel, count, slots, taps.shape[0]),
        out_shape=jax.ShapeDtypeStruct((2, count * slots, LANES, inputs_local), jnp.bfloat16),
        in_specs=[vmem, vmem, pl.BlockSpec(memory_space=pl.ANY)],
        out_specs=vmem,
        scratch_shapes=[
            pltpu.VMEM((CHUNKS, count, slots, rows, frame_len), jnp.bfloat16),
            pltpu.VMEM((4, half, half), jnp.bfloat16),
            pltpu.VMEM((4, all_rows, half), jnp.bfloat16),
            pltpu.VMEM((count, CHUNKS, 2, all_rows, LANES), jnp.bfloat16),
            pltpu.VMEM((count, CHUNKS, 2, all_rows, LANES), jnp.bfloat16),
            pltpu.SemaphoreType.DMA,
            pltpu.SemaphoreType.DMA((CHUNKS, count - 1)),
            pltpu.SemaphoreType.DMA((CHUNKS, count - 1)),
            pltpu.SemaphoreType.DMA((CHUNKS, count - 1)),
            pltpu.SemaphoreType.DMA((CHUNKS, count - 1)),
        ],
        compiler_params=pltpu.CompilerParams(
            collective_id=0, has_side_effects=True, vmem_limit_bytes=48 * 1024 * 1024
        ),
        name="channelize",
    )(volts, taps, table)
    spectra = spectra.reshape(2, count * slots, 2, LANES // 2, inputs_local)
    spectra = jnp.transpose(spectra, (3, 0, 1, 2, 4))
    return spectra.reshape(LANES, count * slots, 2, inputs_local)


def subspace_kernel(
    own_ref, keep_ref, ritz_ref, gram_ref, from_core, from_chip, send_sem, recv_sem
):
    me = lax.axis_index("inp")
    core = lax.rem(me, 2)
    other_core = me + 1 - 2 * core
    other_chip = lax.rem(me + 2, 4)
    barrier = pltpu.get_barrier_semaphore()
    for peer in (other_core, other_chip):
        pl.semaphore_signal(barrier, inc=1, device_id={"inp": peer}, device_id_type=MESH)
    pl.semaphore_wait(barrier, 2)
    rows = from_core.shape[0]
    mine, other = pl.ds(core * rows, rows), pl.ds((1 - core) * rows, rows)

    def exchange(phase, source, target, peer):
        copy = pltpu.make_async_remote_copy(
            src_ref=source,
            dst_ref=target,
            send_sem=send_sem.at[phase],
            recv_sem=recv_sem.at[phase],
            device_id={"inp": peer},
            device_id_type=MESH,
        )
        copy.start()
        copy.wait()

    exchange(0, own_ref.at[other], from_core, other_core)
    gram_ref[mine] = own_ref[mine] + from_core[...]
    exchange(1, gram_ref.at[mine], from_chip, other_chip)
    gram_ref[mine] = gram_ref[mine] + from_chip[...]
    exchange(2, gram_ref.at[mine], gram_ref.at[mine], other_core)
    block = ritz_ref.shape[0]
    frames = keep_ref.shape[0]

    def times_gram(left):
        total = left[:, 0:1] * gram_ref[block][None]
        for frame in range(1, frames):
            total = total + left[:, frame : frame + 1] * gram_ref[block + frame][None]
        return total

    projected = gram_ref[:block]
    coefficients = None
    for iteration in range(ITERS):
        mapped = projected * (1.0 / frames)
        spread = times_gram(mapped)
        columns = [jnp.sum(spread * mapped[k][None], axis=1) for k in range(block)]
        remaining = [mapped[k] for k in range(block)]
        for k in range(block):
            inverse = lax.rsqrt(columns[k][k : k + 1])
            inverse = inverse * (1.5 - 0.5 * columns[k][k : k + 1] * inverse * inverse)
            factor = columns[k] * inverse
            remaining[k] = remaining[k] * inverse
            for j in range(k + 1, block):
                remaining[j] = remaining[j] - factor[j : j + 1] * remaining[k]
                columns[j] = columns[j] - factor[j : j + 1] * factor
        coefficients = jnp.stack(remaining)
        projected = times_gram(coefficients)
    for k in range(block):
        ritz_ref[k] = jnp.sum(projected * projected[k][None], axis=1) * (1.0 / frames)
    row = lax.broadcasted_iota(jnp.int32, keep_ref.shape[1:], 0)
    for frame in range(frames):
        removed = projected[0][frame : frame + 1] * coefficients[0]
        for k in range(1, block):
            removed = removed + projected[k][frame : frame + 1] * coefficients[k]
        keep_ref[frame] = jnp.where(row == frame, 1.0, 0.0) - removed


def clean(turned, start_local):
    channels, frames, parts, inputs_local = turned.shape
    block = start_local.shape[0]
    data = turned.reshape(channels, frames, parts * inputs_local)
    begin = start_local.reshape(block, parts * inputs_local).astype(jnp.bfloat16)
    stacked = jnp.concatenate(
        [jnp.broadcast_to(begin[None], (channels,) + begin.shape), data], axis=1
    )
    gram = jnp.einsum("czr,cmr->czm", stacked, data, preferred_element_type=jnp.float32)
    gram = jnp.transpose(gram, (1, 2, 0))
    half = ((block + frames) // 2, frames, channels)
    keep, ritz = pl.pallas_call(
        subspace_kernel,
        out_shape=(
            jax.ShapeDtypeStruct((frames, frames, channels), jnp.float32),
            jax.ShapeDtypeStruct((block, block, channels), jnp.float32),
        ),
        scratch_shapes=[
            pltpu.VMEM(gram.shape, jnp.float32),
            pltpu.VMEM(half, jnp.float32),
            pltpu.VMEM(half, jnp.float32),
            pltpu.SemaphoreType.DMA((3,)),
            pltpu.SemaphoreType.DMA((3,)),
        ],
        compiler_params=pltpu.CompilerParams(
            collective_id=1, has_side_effects=True, vmem_limit_bytes=32 * 1024 * 1024
        ),
        name="subspace",
    )(gram)
    keep = jnp.transpose(keep, (2, 0, 1))
    cleaned = jnp.einsum(
        "cmn,cnr->cmr", keep, data.astype(jnp.float32), precision=lax.Precision.HIGHEST
    )
    cleaned = cleaned.astype(jnp.bfloat16).reshape(turned.shape)
    return cleaned, jnp.transpose(ritz, (2, 0, 1))


def from_behind(value, axis, steps):
    count = lax.axis_size(axis)
    pairs = [(source, (source + steps) % count) for source in range(count)]
    return lax.ppermute(value, axis, pairs)


def project_rows(basis_rows, channel_data):
    projected = jnp.einsum(
        "ckr,cmr->ckm", basis_rows, channel_data, precision=lax.Precision.HIGHEST
    )
    return lax.psum(projected, "inp")


def subspace_clean(turned, start_block):
    highest = lax.Precision.HIGHEST
    channel_local, spectra_count, part_count, inputs_width = turned.shape
    row_count = part_count * inputs_width
    channel_data = turned.reshape(channel_local, spectra_count, row_count).astype(jnp.float32)
    start_rows = start_block.reshape(start_block.shape[0], row_count).astype(jnp.float32)
    basis_rows = jnp.broadcast_to(start_rows[None], (channel_local,) + start_rows.shape)
    for iteration in range(ITERS):
        projected = project_rows(basis_rows, channel_data)
        mapped = (
            jnp.einsum("ckm,cmr->ckr", projected, channel_data, precision=highest) / spectra_count
        )
        gram_matrix = jnp.einsum("ckr,cjr->ckj", mapped, mapped, precision=highest)
        gram_matrix = lax.psum(gram_matrix, "inp")
        lower_factor = jnp.linalg.cholesky(gram_matrix)
        basis_rows = lax.linalg.triangular_solve(lower_factor, mapped, left_side=True, lower=True)
    projected = project_rows(basis_rows, channel_data)
    ritz_matrix = (
        jnp.einsum("ckm,cjm->ckj", projected, projected, precision=highest) / spectra_count
    )
    cleaned = channel_data - jnp.einsum("ckm,ckr->cmr", projected, basis_rows, precision=highest)
    cleaned = cleaned.reshape(channel_local, spectra_count, part_count, inputs_width).astype(
        jnp.bfloat16
    )
    return (cleaned, ritz_matrix)


def general_shards(voltages, taps, start):
    slot_count = voltages.shape[0]
    frame_len = voltages.shape[1]
    inputs_local = voltages.shape[2]
    channel_count = frame_len // 2
    tap_count = taps.shape[0]
    frame_stack = voltages.astype(jnp.bfloat16)
    history_len = tap_count - 1
    group_count = lax.axis_size("freq")
    portions = [frame_stack]
    shift_count = (history_len - 1) // slot_count + 1
    for distance in range(1, shift_count + 1):
        first_frame = max(0, distance * slot_count - history_len)
        portion = frame_stack[first_frame:]
        offset_mod = distance % group_count
        arrived = from_behind(portion, "freq", offset_mod)
        portions = [arrived] + portions
    extended = jnp.concatenate(portions, axis=0)
    filtered = jnp.zeros((slot_count, frame_len, inputs_local), jnp.float32)
    for tap_index in range(tap_count):
        window = extended[tap_index : tap_index + slot_count].astype(jnp.float32)
        filtered = filtered + taps[tap_index][None, :, None] * window
    channel_idx = lax.broadcasted_iota(jnp.int32, (channel_count, frame_len), 0)
    sample_idx = lax.broadcasted_iota(jnp.int32, (channel_count, frame_len), 1)
    angles = (channel_idx * sample_idx % frame_len).astype(jnp.float32) * (
        2.0 * math.pi / frame_len
    )
    dft_scale = 1.0 / math.sqrt(channel_count)
    cosine = jnp.cos(angles)
    sine_table = jnp.sin(angles)
    real_part = (
        jnp.einsum("kn,sni->ksi", cosine, filtered, precision=lax.Precision.HIGHEST) * dft_scale
    )
    imag_part = (
        -jnp.einsum("kn,sni->ksi", sine_table, filtered, precision=lax.Precision.HIGHEST)
        * dft_scale
    )
    spectra = jnp.stack([real_part, imag_part], axis=2).astype(jnp.bfloat16)
    turned = lax.all_to_all(spectra, "freq", split_axis=0, concat_axis=1, tiled=True)
    start_local = lax.dynamic_slice_in_dim(
        start, lax.axis_index("inp") * inputs_local, inputs_local, 2
    )
    cleaned, ritz_matrix = subspace_clean(turned, start_local)
    return (cleaned, ritz_matrix)


def start_columns(start, inputs_local):
    return lax.dynamic_slice_in_dim(start, lax.axis_index("inp") * inputs_local, inputs_local, 2)


def shards(voltages, taps, start):
    slots, frame_len, inputs_local = voltages.shape
    count = lax.axis_size("freq")
    fits = (
        count % 2 == 0
        and lax.axis_size("inp") == 4
        and (count * slots + start.shape[0]) % 2 == 0
        and frame_len // 2 == count * LANES
        and inputs_local == CHUNKS * LANES
        and LANES % (count * 16) == 0
        and count * slots <= 32
        and taps.shape[0] <= count * slots
    )
    if not fits:
        return general_shards(voltages, taps, start)
    return clean(channelize(voltages, taps), start_columns(start, inputs_local))


def solution(mesh):
    placed = (P("freq", None, "inp"), P(), P())
    return jax.shard_map(
        shards,
        mesh=mesh,
        in_specs=placed,
        out_specs=(P("freq", None, None, "inp"), P("freq", None, None)),
        check_vma=False,
    )
```

```python
import functools
import math

import jax
import jax.numpy as jnp
import ml_dtypes
import numpy as np
from jax import lax
from jax.experimental import pallas as pl
from jax.experimental.pallas import tpu as pltpu
from jax.sharding import PartitionSpec as P

ITERS = 4
CHUNKS = 2
LANES = 128
MESH = pl.DeviceIdType.MESH


def dft_tables(frame_len, group_count):
    half = frame_len // 2
    pairs = half // 2
    sample = np.arange(half, dtype=np.int64)[:, None]
    tables = []
    for parity in (0, 1):
        channel = 2 * np.arange(pairs, dtype=np.int64)[None, :] + parity
        angle = 2.0 * np.pi * ((sample * channel) % frame_len) / frame_len
        scale = 1.0 / math.sqrt(half)
        real = (np.cos(angle) * scale).reshape(half, group_count, 1, pairs // group_count)
        imag = (-np.sin(angle) * scale).reshape(half, group_count, 1, pairs // group_count)
        table = np.concatenate([real, imag], axis=2).reshape(half, half)
        high = table.astype(ml_dtypes.bfloat16)
        low = (table - high.astype(np.float64)).astype(ml_dtypes.bfloat16)
        tables += [high, low]
    return np.stack(tables)


def channelize_kernel(
    count, slots, tap_count, raw_hbm, taps_ref, table_hbm, spectra_ref,
    raw, volts_ref, gathered, table, halves, outgoing, landed,
    raw_sem, table_sem, send_a, recv_a, send_b, recv_b,
):
    me = lax.axis_index("freq")
    frames = count * slots
    half = table.shape[1]
    rows = volts_ref.shape[3]

    raw_copies = [
        pltpu.make_async_copy(
            raw_hbm.at[:, :, chunk * LANES : (chunk + 1) * LANES], raw.at[chunk], raw_sem.at[chunk]
        )
        for chunk in range(CHUNKS)
    ]
    for copy in raw_copies:
        copy.start()
    table_copy = pltpu.make_async_copy(table_hbm, table, table_sem)
    table_copy.start()
    barrier = pltpu.get_barrier_semaphore()
    for step in range(1, count):
        peer = lax.rem(me + step, count)
        pl.semaphore_signal(barrier, inc=1, device_id={"freq": peer}, device_id_type=MESH)

    def turn_input(chunk):
        raw_copies[chunk].wait()
        width = 2 * LANES
        tiles = 2 * half // width

        def turn_tile(index, carry):
            frame, tile = lax.div(index, tiles), lax.rem(index, tiles)
            at = pl.ds(pl.multiple_of(tile * width, width), width)
            block = raw[chunk, frame, at, :].astype(jnp.float32).astype(jnp.bfloat16)
            volts_ref[:, chunk, frame, :, at] = block.T.reshape(count, rows, width)
            return carry

        lax.fori_loop(0, slots * tiles, turn_tile, 0)

    turn_input(0)
    pl.semaphore_wait(barrier, count - 1)

    def voltage_copy(chunk, step):
        peer = lax.rem(me + step, count)
        return pltpu.make_async_remote_copy(
            src_ref=volts_ref.at[peer, chunk],
            dst_ref=gathered.at[chunk, me],
            send_sem=send_a.at[chunk, step - 1],
            recv_sem=recv_a.at[chunk, step - 1],
            device_id={"freq": peer},
            device_id_type=MESH,
        )

    def spectra_copy(chunk, step):
        peer = lax.rem(me + step, count)
        return pltpu.make_async_remote_copy(
            src_ref=outgoing.at[peer, chunk],
            dst_ref=landed.at[me, chunk],
            send_sem=send_b.at[chunk, step - 1],
            recv_sem=recv_b.at[chunk, step - 1],
            device_id={"freq": peer},
            device_id_type=MESH,
        )

    order = sorted(range(1, count), key=lambda step: -min(step, count - step))
    for step in order:
        voltage_copy(0, step).start()
    gathered[0, me] = volts_ref[me, 0]
    for chunk in range(1, CHUNKS):
        turn_input(chunk)
        gathered[chunk, me] = volts_ref[me, chunk]
    for chunk in range(CHUNKS):
        if chunk == 0:
            for step in order:
                voltage_copy(0, step).wait_send()
                voltage_copy(1, step).start()
        for step in order:
            voltage_copy(chunk, step).wait_recv()

        def filter_tile(tile, carry):
            sums = []
            for part in (0, 1):
                at = pl.ds(pl.multiple_of(tile * LANES + part * half, LANES), LANES)
                window = gathered[chunk, :, :, :, at].astype(jnp.float32)
                window = window.reshape(frames, rows, LANES)
                extended = jnp.concatenate([window[frames - tap_count + 1 :], window], axis=0)
                total = taps_ref[0:1, at][None] * extended[:frames]
                for tap in range(1, tap_count):
                    total = total + taps_ref[tap : tap + 1, at][None] * extended[tap : tap + frames]
                sums.append(total.reshape(frames * rows, LANES))
            at = pl.ds(pl.multiple_of(tile * LANES, LANES), LANES)
            for index, value in ((0, sums[0] + sums[1]), (2, sums[0] - sums[1])):
                high = value.astype(jnp.bfloat16)
                halves[index, :, at] = high
                halves[index + 1, :, at] = (value - high.astype(jnp.float32)).astype(jnp.bfloat16)
            return carry

        lax.fori_loop(0, half // LANES, filter_tile, 0)
        if chunk == 0:
            table_copy.wait()

        def transform_tile(pair, carry):
            at = pl.ds(pl.multiple_of(pair * 2 * LANES, 2 * LANES), 2 * LANES)
            for parity in (0, 1):
                high, low = halves[2 * parity], halves[2 * parity + 1]
                table_high = table[2 * parity, :, at]
                table_low = table[2 * parity + 1, :, at]
                dot = functools.partial(jnp.dot, preferred_element_type=jnp.float32)
                result = dot(low, table_high) + dot(high, table_low) + dot(high, table_high)
                result = result.astype(jnp.bfloat16)
                outgoing[2 * pair, chunk, parity] = result[:, :LANES]
                outgoing[2 * pair + 1, chunk, parity] = result[:, LANES:]
            return carry

        lax.fori_loop(0, count // 2, transform_tile, 0)
        for step in order:
            if chunk == 0:
                voltage_copy(1, step).wait_send()
            spectra_copy(chunk, step).start()
        landed[me, chunk] = outgoing[me, chunk]
    for chunk in range(CHUNKS):
        for step in order:
            spectra_copy(chunk, step).wait()

        def turn_frame(index, carry):
            parity, frame = lax.div(index, frames), lax.rem(index, frames)
            at = pl.ds(pl.multiple_of(frame * rows, rows), rows)
            block = landed[:, chunk, parity, at, :].reshape(count * rows, LANES)
            block = block.T
            for part in (0, 1):
                spectra_ref[parity, part, frame, :, chunk * LANES : (chunk + 1) * LANES] = block[
                    part * LANES // 2 : (part + 1) * LANES // 2
                ]
            return carry

        lax.fori_loop(0, 2 * frames, turn_frame, 0)


def channelize(voltages, taps):
    slots, frame_len, inputs_local = voltages.shape
    count = lax.axis_size("freq")
    half = frame_len // 2
    rows = inputs_local // (count * CHUNKS)
    table = jnp.asarray(dft_tables(frame_len, count))
    all_rows = count * slots * rows
    vmem = pl.BlockSpec(memory_space=pltpu.VMEM)
    spectra = pl.pallas_call(
        functools.partial(channelize_kernel, count, slots, taps.shape[0]),
        out_shape=jax.ShapeDtypeStruct((2, 2, count * slots, LANES // 2, inputs_local), jnp.bfloat16),
        in_specs=[pl.BlockSpec(memory_space=pl.ANY), vmem, pl.BlockSpec(memory_space=pl.ANY)],
        out_specs=vmem,
        scratch_shapes=[
            pltpu.VMEM((CHUNKS, slots, frame_len, LANES), voltages.dtype),
            pltpu.VMEM((count, CHUNKS, slots, rows, frame_len), jnp.bfloat16),
            pltpu.VMEM((CHUNKS, count, slots, rows, frame_len), jnp.bfloat16),
            pltpu.VMEM((4, half, half), jnp.bfloat16),
            pltpu.VMEM((4, all_rows, half), jnp.bfloat16),
            pltpu.VMEM((count, CHUNKS, 2, all_rows, LANES), jnp.bfloat16),
            pltpu.VMEM((count, CHUNKS, 2, all_rows, LANES), jnp.bfloat16),
            pltpu.SemaphoreType.DMA((CHUNKS,)),
            pltpu.SemaphoreType.DMA,
            pltpu.SemaphoreType.DMA((CHUNKS, count - 1)),
            pltpu.SemaphoreType.DMA((CHUNKS, count - 1)),
            pltpu.SemaphoreType.DMA((CHUNKS, count - 1)),
            pltpu.SemaphoreType.DMA((CHUNKS, count - 1)),
        ],
        compiler_params=pltpu.CompilerParams(
            collective_id=0, has_side_effects=True, vmem_limit_bytes=48 * 1024 * 1024
        ),
        name="channelize",
    )(voltages, taps, table)
    spectra = jnp.transpose(spectra, (3, 0, 1, 2, 4))
    return spectra.reshape(LANES, 2, count * slots, inputs_local)


def subspace_kernel(
    own_ref, keep_ref, ritz_ref, gram_ref, from_core, from_chip, send_sem, recv_sem
):
    me = lax.axis_index("inp")
    core = lax.rem(me, 2)
    other_core = me + 1 - 2 * core
    other_chip = lax.rem(me + 2, 4)
    barrier = pltpu.get_barrier_semaphore()
    for peer in (other_core, other_chip):
        pl.semaphore_signal(barrier, inc=1, device_id={"inp": peer}, device_id_type=MESH)
    pl.semaphore_wait(barrier, 2)
    rows = from_core.shape[0]
    mine, other = pl.ds(core * rows, rows), pl.ds((1 - core) * rows, rows)

    def exchange(phase, source, target, peer):
        copy = pltpu.make_async_remote_copy(
            src_ref=source,
            dst_ref=target,
            send_sem=send_sem.at[phase],
            recv_sem=recv_sem.at[phase],
            device_id={"inp": peer},
            device_id_type=MESH,
        )
        copy.start()
        copy.wait()

    exchange(0, own_ref.at[other], from_core, other_core)
    gram_ref[mine] = own_ref[mine] + from_core[...]
    exchange(1, gram_ref.at[mine], from_chip, other_chip)
    gram_ref[mine] = gram_ref[mine] + from_chip[...]
    exchange(2, gram_ref.at[mine], gram_ref.at[mine], other_core)
    block = ritz_ref.shape[0]
    frames = keep_ref.shape[0]

    def times_gram(left):
        total = left[:, 0:1] * gram_ref[block][None]
        for frame in range(1, frames):
            total = total + left[:, frame : frame + 1] * gram_ref[block + frame][None]
        return total

    projected = gram_ref[:block]
    coefficients = None
    for iteration in range(ITERS):
        mapped = projected * (1.0 / frames)
        spread = times_gram(mapped)
        columns = [jnp.sum(spread * mapped[k][None], axis=1) for k in range(block)]
        remaining = [mapped[k] for k in range(block)]
        for k in range(block):
            inverse = lax.rsqrt(columns[k][k : k + 1])
            inverse = inverse * (1.5 - 0.5 * columns[k][k : k + 1] * inverse * inverse)
            factor = columns[k] * inverse
            remaining[k] = remaining[k] * inverse
            for j in range(k + 1, block):
                remaining[j] = remaining[j] - factor[j : j + 1] * remaining[k]
                columns[j] = columns[j] - factor[j : j + 1] * factor
        coefficients = jnp.stack(remaining)
        projected = times_gram(coefficients)
    for k in range(block):
        ritz_ref[k] = jnp.sum(projected * projected[k][None], axis=1) * (1.0 / frames)
    row = lax.broadcasted_iota(jnp.int32, keep_ref.shape[1:], 0)
    for frame in range(frames):
        removed = projected[0][frame : frame + 1] * coefficients[0]
        for k in range(1, block):
            removed = removed + projected[k][frame : frame + 1] * coefficients[k]
        keep_ref[frame] = jnp.where(row == frame, 1.0, 0.0) - removed


def clean(turned, start_local):
    channels, parts, frames, inputs_local = turned.shape
    block = start_local.shape[0]
    begin = jnp.swapaxes(start_local, 0, 1).astype(jnp.bfloat16)
    stacked = jnp.concatenate(
        [jnp.broadcast_to(begin[None], (channels,) + begin.shape), turned], axis=2
    )
    gram = jnp.einsum("cqzi,cqmi->cqzm", stacked, turned, preferred_element_type=jnp.float32)
    gram = jnp.transpose(jnp.sum(gram, axis=1), (1, 2, 0))
    half = ((block + frames) // 2, frames, channels)
    keep, ritz = pl.pallas_call(
        subspace_kernel,
        out_shape=(
            jax.ShapeDtypeStruct((frames, frames, channels), jnp.float32),
            jax.ShapeDtypeStruct((block, block, channels), jnp.float32),
        ),
        scratch_shapes=[
            pltpu.VMEM(gram.shape, jnp.float32),
            pltpu.VMEM(half, jnp.float32),
            pltpu.VMEM(half, jnp.float32),
            pltpu.SemaphoreType.DMA((3,)),
            pltpu.SemaphoreType.DMA((3,)),
        ],
        compiler_params=pltpu.CompilerParams(
            collective_id=1, has_side_effects=True, vmem_limit_bytes=32 * 1024 * 1024
        ),
        name="subspace",
    )(gram)
    keep = jnp.transpose(keep, (2, 0, 1))
    keep = jnp.broadcast_to(keep[:, None], (channels, parts, frames, frames))
    cleaned = jnp.einsum(
        "cqmn,cqni->cqmi", keep, turned.astype(jnp.float32), precision=lax.Precision.HIGHEST
    )
    cleaned = jnp.swapaxes(cleaned.astype(jnp.bfloat16), 1, 2)
    return cleaned, jnp.transpose(ritz, (2, 0, 1))


def from_behind(value, axis, steps):
    count = lax.axis_size(axis)
    pairs = [(source, (source + steps) % count) for source in range(count)]
    return lax.ppermute(value, axis, pairs)


def project_rows(basis_rows, channel_data):
    projected = jnp.einsum(
        "ckr,cmr->ckm", basis_rows, channel_data, precision=lax.Precision.HIGHEST
    )
    return lax.psum(projected, "inp")


def subspace_clean(turned, start_block):
    highest = lax.Precision.HIGHEST
    channel_local, spectra_count, part_count, inputs_width = turned.shape
    row_count = part_count * inputs_width
    channel_data = turned.reshape(channel_local, spectra_count, row_count).astype(jnp.float32)
    start_rows = start_block.reshape(start_block.shape[0], row_count).astype(jnp.float32)
    basis_rows = jnp.broadcast_to(start_rows[None], (channel_local,) + start_rows.shape)
    for iteration in range(ITERS):
        projected = project_rows(basis_rows, channel_data)
        mapped = (
            jnp.einsum("ckm,cmr->ckr", projected, channel_data, precision=highest) / spectra_count
        )
        gram_matrix = jnp.einsum("ckr,cjr->ckj", mapped, mapped, precision=highest)
        gram_matrix = lax.psum(gram_matrix, "inp")
        lower_factor = jnp.linalg.cholesky(gram_matrix)
        basis_rows = lax.linalg.triangular_solve(lower_factor, mapped, left_side=True, lower=True)
    projected = project_rows(basis_rows, channel_data)
    ritz_matrix = (
        jnp.einsum("ckm,cjm->ckj", projected, projected, precision=highest) / spectra_count
    )
    cleaned = channel_data - jnp.einsum("ckm,ckr->cmr", projected, basis_rows, precision=highest)
    cleaned = cleaned.reshape(channel_local, spectra_count, part_count, inputs_width).astype(
        jnp.bfloat16
    )
    return (cleaned, ritz_matrix)


def general_shards(voltages, taps, start):
    slot_count = voltages.shape[0]
    frame_len = voltages.shape[1]
    inputs_local = voltages.shape[2]
    channel_count = frame_len // 2
    tap_count = taps.shape[0]
    frame_stack = voltages.astype(jnp.bfloat16)
    history_len = tap_count - 1
    group_count = lax.axis_size("freq")
    portions = [frame_stack]
    shift_count = (history_len - 1) // slot_count + 1
    for distance in range(1, shift_count + 1):
        first_frame = max(0, distance * slot_count - history_len)
        portion = frame_stack[first_frame:]
        offset_mod = distance % group_count
        arrived = from_behind(portion, "freq", offset_mod)
        portions = [arrived] + portions
    extended = jnp.concatenate(portions, axis=0)
    filtered = jnp.zeros((slot_count, frame_len, inputs_local), jnp.float32)
    for tap_index in range(tap_count):
        window = extended[tap_index : tap_index + slot_count].astype(jnp.float32)
        filtered = filtered + taps[tap_index][None, :, None] * window
    channel_idx = lax.broadcasted_iota(jnp.int32, (channel_count, frame_len), 0)
    sample_idx = lax.broadcasted_iota(jnp.int32, (channel_count, frame_len), 1)
    angles = (channel_idx * sample_idx % frame_len).astype(jnp.float32) * (
        2.0 * math.pi / frame_len
    )
    dft_scale = 1.0 / math.sqrt(channel_count)
    cosine = jnp.cos(angles)
    sine_table = jnp.sin(angles)
    real_part = (
        jnp.einsum("kn,sni->ksi", cosine, filtered, precision=lax.Precision.HIGHEST) * dft_scale
    )
    imag_part = (
        -jnp.einsum("kn,sni->ksi", sine_table, filtered, precision=lax.Precision.HIGHEST)
        * dft_scale
    )
    spectra = jnp.stack([real_part, imag_part], axis=2).astype(jnp.bfloat16)
    turned = lax.all_to_all(spectra, "freq", split_axis=0, concat_axis=1, tiled=True)
    start_local = lax.dynamic_slice_in_dim(
        start, lax.axis_index("inp") * inputs_local, inputs_local, 2
    )
    cleaned, ritz_matrix = subspace_clean(turned, start_local)
    return (cleaned, ritz_matrix)


def start_columns(start, inputs_local):
    return lax.dynamic_slice_in_dim(start, lax.axis_index("inp") * inputs_local, inputs_local, 2)


def shards(voltages, taps, start):
    slots, frame_len, inputs_local = voltages.shape
    count = lax.axis_size("freq")
    fits = (
        count % 2 == 0
        and lax.axis_size("inp") == 4
        and (count * slots + start.shape[0]) % 2 == 0
        and frame_len // 2 == count * LANES
        and inputs_local == CHUNKS * LANES
        and LANES % (count * 16) == 0
        and count * slots <= 32
        and taps.shape[0] <= count * slots
    )
    if not fits:
        return general_shards(voltages, taps, start)
    return clean(channelize(voltages, taps), start_columns(start, inputs_local))


def solution(mesh):
    placed = (P("freq", None, "inp"), P(), P())
    return jax.shard_map(
        shards,
        mesh=mesh,
        in_specs=placed,
        out_specs=(P("freq", None, None, "inp"), P("freq", None, None)),
        check_vma=False,
    )
```

```python
import functools
import math

import jax
import jax.numpy as jnp
import ml_dtypes
import numpy as np
from jax import lax
from jax.experimental import pallas as pl
from jax.experimental.pallas import tpu as pltpu
from jax.sharding import PartitionSpec as P

ITERS = 4
CHUNKS = 2
LANES = 128
MESH = pl.DeviceIdType.MESH


def dft_tables(frame_len, group_count):
    half = frame_len // 2
    pairs = half // 2
    sample = np.arange(half, dtype=np.int64)[:, None]
    tables = []
    for parity in (0, 1):
        channel = 2 * np.arange(pairs, dtype=np.int64)[None, :] + parity
        angle = 2.0 * np.pi * ((sample * channel) % frame_len) / frame_len
        scale = 1.0 / math.sqrt(half)
        real = (np.cos(angle) * scale).reshape(half, group_count, 1, pairs // group_count)
        imag = (-np.sin(angle) * scale).reshape(half, group_count, 1, pairs // group_count)
        table = np.concatenate([real, imag], axis=2).reshape(half, half)
        high = table.astype(ml_dtypes.bfloat16)
        low = (table - high.astype(np.float64)).astype(ml_dtypes.bfloat16)
        tables += [high, low]
    return np.stack(tables)


def channelize_kernel(
    count, slots, tap_count, raw_hbm, taps_ref, table_hbm, spectra_ref,
    raw, volts_ref, gathered, table, halves, outgoing, landed,
    raw_sem, table_sem, send_a, recv_a, send_b, recv_b,
):
    me = lax.axis_index("freq")
    frames = count * slots
    half = table.shape[1]
    rows = volts_ref.shape[3]

    raw_copies = [
        pltpu.make_async_copy(
            raw_hbm.at[:, :, chunk * LANES : (chunk + 1) * LANES], raw.at[chunk], raw_sem.at[chunk]
        )
        for chunk in range(CHUNKS)
    ]
    raw_copies[0].start()
    table_copy = pltpu.make_async_copy(table_hbm, table, table_sem)
    barrier = pltpu.get_barrier_semaphore()
    for step in range(1, count):
        peer = lax.rem(me + step, count)
        pl.semaphore_signal(barrier, inc=1, device_id={"freq": peer}, device_id_type=MESH)

    def turn_input(chunk, frame):
        width = 2 * LANES

        def turn_tile(tile, carry):
            at = pl.ds(pl.multiple_of(tile * width, width), width)
            block = raw[chunk, frame, at, :].astype(jnp.float32).astype(jnp.bfloat16)
            volts_ref[:, chunk, frame, :, at] = block.T.reshape(count, rows, width)
            return carry

        lax.fori_loop(0, 2 * half // width, turn_tile, 0)

    def voltage_copy(chunk, step, frame):
        peer = lax.rem(me + step, count)
        return pltpu.make_async_remote_copy(
            src_ref=volts_ref.at[peer, chunk, frame],
            dst_ref=gathered.at[chunk, me, frame],
            send_sem=send_a.at[chunk, frame, step - 1],
            recv_sem=recv_a.at[chunk, frame, step - 1],
            device_id={"freq": peer},
            device_id_type=MESH,
        )

    def spectra_copy(chunk, step, parity):
        peer = lax.rem(me + step, count)
        return pltpu.make_async_remote_copy(
            src_ref=outgoing.at[peer, chunk, parity],
            dst_ref=landed.at[me, chunk, parity],
            send_sem=send_b.at[chunk, parity, step - 1],
            recv_sem=recv_b.at[chunk, parity, step - 1],
            device_id={"freq": peer},
            device_id_type=MESH,
        )

    order = sorted(range(1, count), key=lambda step: -min(step, count - step))
    raw_copies[0].wait()
    raw_copies[1].start()
    table_copy.start()
    for frame in range(slots):
        turn_input(0, frame)
        if frame == 0:
            pl.semaphore_wait(barrier, count - 1)
        for step in order:
            voltage_copy(0, step, frame).start()
    raw_copies[1].wait()
    for frame in range(slots):
        turn_input(1, frame)
    for chunk in range(CHUNKS):
        gathered[chunk, me] = volts_ref[me, chunk]
    for chunk in range(CHUNKS):
        if chunk == 0:
            for frame in range(slots):
                for step in order:
                    voltage_copy(0, step, frame).wait_send()
                    voltage_copy(1, step, frame).start()
        for frame in range(slots):
            for step in order:
                voltage_copy(chunk, step, frame).wait_recv()

        def filter_tile(tile, carry):
            sums = []
            for part in (0, 1):
                at = pl.ds(pl.multiple_of(tile * LANES + part * half, LANES), LANES)
                window = gathered[chunk, :, :, :, at].astype(jnp.float32)
                window = window.reshape(frames, rows, LANES)
                extended = jnp.concatenate([window[frames - tap_count + 1 :], window], axis=0)
                total = taps_ref[0:1, at][None] * extended[:frames]
                for tap in range(1, tap_count):
                    total = total + taps_ref[tap : tap + 1, at][None] * extended[tap : tap + frames]
                sums.append(total.reshape(frames * rows, LANES))
            at = pl.ds(pl.multiple_of(tile * LANES, LANES), LANES)
            for index, value in ((0, sums[0] + sums[1]), (2, sums[0] - sums[1])):
                high = value.astype(jnp.bfloat16)
                halves[index, :, at] = high
                halves[index + 1, :, at] = (value - high.astype(jnp.float32)).astype(jnp.bfloat16)
            return carry

        lax.fori_loop(0, half // LANES, filter_tile, 0)
        if chunk == 0:
            table_copy.wait()

        def transform_tile(pair, carry):
            at = pl.ds(pl.multiple_of(pair * 2 * LANES, 2 * LANES), 2 * LANES)
            for parity in (0, 1):
                high, low = halves[2 * parity], halves[2 * parity + 1]
                table_high = table[2 * parity, :, at]
                table_low = table[2 * parity + 1, :, at]
                dot = functools.partial(jnp.dot, preferred_element_type=jnp.float32)
                result = dot(low, table_high) + dot(high, table_low) + dot(high, table_high)
                result = result.astype(jnp.bfloat16)
                outgoing[2 * pair, chunk, parity] = result[:, :LANES]
                outgoing[2 * pair + 1, chunk, parity] = result[:, LANES:]
            return carry

        lax.fori_loop(0, count // 2, transform_tile, 0)
        for step in order:
            for frame in range(slots if chunk == 0 else 0):
                voltage_copy(1, step, frame).wait_send()
            spectra_copy(chunk, step, 0).start()
        for step in order:
            spectra_copy(chunk, step, 1).start()
        landed[me, chunk] = outgoing[me, chunk]
    for chunk in range(CHUNKS):
        for parity in (0, 1):
            for step in order:
                spectra_copy(chunk, step, parity).wait()

            def turn_frame(frame, carry):
                at = pl.ds(pl.multiple_of(frame * rows, rows), rows)
                block = landed[:, chunk, parity, at, :].reshape(count * rows, LANES).T
                for part in (0, 1):
                    spectra_ref[
                        parity, part, frame, :, chunk * LANES : (chunk + 1) * LANES
                    ] = block[part * LANES // 2 : (part + 1) * LANES // 2]
                return carry

            lax.fori_loop(0, frames, turn_frame, 0)


def channelize(voltages, taps):
    slots, frame_len, inputs_local = voltages.shape
    count = lax.axis_size("freq")
    half = frame_len // 2
    rows = inputs_local // (count * CHUNKS)
    table = jnp.asarray(dft_tables(frame_len, count))
    all_rows = count * slots * rows
    vmem = pl.BlockSpec(memory_space=pltpu.VMEM)
    spectra = pl.pallas_call(
        functools.partial(channelize_kernel, count, slots, taps.shape[0]),
        out_shape=jax.ShapeDtypeStruct((2, 2, count * slots, LANES // 2, inputs_local), jnp.bfloat16),
        in_specs=[pl.BlockSpec(memory_space=pl.ANY), vmem, pl.BlockSpec(memory_space=pl.ANY)],
        out_specs=vmem,
        scratch_shapes=[
            pltpu.VMEM((CHUNKS, slots, frame_len, LANES), voltages.dtype),
            pltpu.VMEM((count, CHUNKS, slots, rows, frame_len), jnp.bfloat16),
            pltpu.VMEM((CHUNKS, count, slots, rows, frame_len), jnp.bfloat16),
            pltpu.VMEM((4, half, half), jnp.bfloat16),
            pltpu.VMEM((4, all_rows, half), jnp.bfloat16),
            pltpu.VMEM((count, CHUNKS, 2, all_rows, LANES), jnp.bfloat16),
            pltpu.VMEM((count, CHUNKS, 2, all_rows, LANES), jnp.bfloat16),
            pltpu.SemaphoreType.DMA((CHUNKS,)),
            pltpu.SemaphoreType.DMA,
            pltpu.SemaphoreType.DMA((CHUNKS, slots, count - 1)),
            pltpu.SemaphoreType.DMA((CHUNKS, slots, count - 1)),
            pltpu.SemaphoreType.DMA((CHUNKS, 2, count - 1)),
            pltpu.SemaphoreType.DMA((CHUNKS, 2, count - 1)),
        ],
        compiler_params=pltpu.CompilerParams(
            collective_id=0, has_side_effects=True, vmem_limit_bytes=48 * 1024 * 1024
        ),
        name="channelize",
    )(voltages, taps, table)
    spectra = jnp.transpose(spectra, (3, 0, 1, 2, 4))
    return spectra.reshape(LANES, 2, count * slots, inputs_local)


def subspace_kernel(
    own_ref, keep_ref, ritz_ref, gram_ref, from_core, from_chip, send_sem, recv_sem
):
    me = lax.axis_index("inp")
    core = lax.rem(me, 2)
    other_core = me + 1 - 2 * core
    other_chip = lax.rem(me + 2, 4)
    barrier = pltpu.get_barrier_semaphore()
    for peer in (other_core, other_chip):
        pl.semaphore_signal(barrier, inc=1, device_id={"inp": peer}, device_id_type=MESH)
    pl.semaphore_wait(barrier, 2)
    rows = from_core.shape[0]
    mine, other = pl.ds(core * rows, rows), pl.ds((1 - core) * rows, rows)

    def exchange(phase, source, target, peer):
        copy = pltpu.make_async_remote_copy(
            src_ref=source,
            dst_ref=target,
            send_sem=send_sem.at[phase],
            recv_sem=recv_sem.at[phase],
            device_id={"inp": peer},
            device_id_type=MESH,
        )
        copy.start()
        copy.wait()

    exchange(0, own_ref.at[other], from_core, other_core)
    gram_ref[mine] = own_ref[mine] + from_core[...]
    exchange(1, gram_ref.at[mine], from_chip, other_chip)
    gram_ref[mine] = gram_ref[mine] + from_chip[...]
    exchange(2, gram_ref.at[mine], gram_ref.at[mine], other_core)
    block = ritz_ref.shape[0]
    frames = keep_ref.shape[0]

    def times_gram(left):
        total = left[:, 0:1] * gram_ref[block][None]
        for frame in range(1, frames):
            total = total + left[:, frame : frame + 1] * gram_ref[block + frame][None]
        return total

    projected = gram_ref[:block]
    coefficients = None
    for iteration in range(ITERS):
        mapped = projected * (1.0 / frames)
        spread = times_gram(mapped)
        columns = [jnp.sum(spread * mapped[k][None], axis=1) for k in range(block)]
        remaining = [mapped[k] for k in range(block)]
        for k in range(block):
            inverse = lax.rsqrt(columns[k][k : k + 1])
            inverse = inverse * (1.5 - 0.5 * columns[k][k : k + 1] * inverse * inverse)
            factor = columns[k] * inverse
            remaining[k] = remaining[k] * inverse
            for j in range(k + 1, block):
                remaining[j] = remaining[j] - factor[j : j + 1] * remaining[k]
                columns[j] = columns[j] - factor[j : j + 1] * factor
        coefficients = jnp.stack(remaining)
        projected = times_gram(coefficients)
    for k in range(block):
        ritz_ref[k] = jnp.sum(projected * projected[k][None], axis=1) * (1.0 / frames)
    row = lax.broadcasted_iota(jnp.int32, projected.shape[1:], 0)
    for frame in range(frames):
        removed = projected[0][frame : frame + 1] * coefficients[0]
        for k in range(1, block):
            removed = removed + projected[k][frame : frame + 1] * coefficients[k]
        keep = jnp.where(row == frame, 1.0, 0.0) - removed
        high = keep.astype(jnp.bfloat16).astype(jnp.float32)
        keep_ref[frame, :frames] = high
        keep_ref[frame, frames:] = keep - high


def clean(turned, start_local):
    channels, parts, frames, inputs_local = turned.shape
    block = start_local.shape[0]
    begin = jnp.swapaxes(start_local, 0, 1).astype(jnp.bfloat16)
    stacked = jnp.concatenate(
        [jnp.broadcast_to(begin[None], (channels,) + begin.shape), turned], axis=2
    )
    gram = jnp.einsum("cqzi,cqmi->cqzm", stacked, turned, preferred_element_type=jnp.float32)
    gram = jnp.transpose(jnp.sum(gram, axis=1), (1, 2, 0))
    half = ((block + frames) // 2, frames, channels)
    keep, ritz = pl.pallas_call(
        subspace_kernel,
        out_shape=(
            jax.ShapeDtypeStruct((frames, 2 * frames, channels), jnp.float32),
            jax.ShapeDtypeStruct((block, block, channels), jnp.float32),
        ),
        scratch_shapes=[
            pltpu.VMEM(gram.shape, jnp.float32),
            pltpu.VMEM(half, jnp.float32),
            pltpu.VMEM(half, jnp.float32),
            pltpu.SemaphoreType.DMA((3,)),
            pltpu.SemaphoreType.DMA((3,)),
        ],
        compiler_params=pltpu.CompilerParams(
            collective_id=1, has_side_effects=True, vmem_limit_bytes=32 * 1024 * 1024
        ),
        name="subspace",
    )(gram)
    keep = jnp.transpose(keep, (2, 0, 1)).astype(jnp.bfloat16)
    keep = jnp.broadcast_to(keep[:, None], (channels, parts, frames, 2 * frames))
    twice = jnp.concatenate([turned, turned], axis=2)
    cleaned = jnp.einsum("cqmn,cqni->cqmi", keep, twice, preferred_element_type=jnp.float32)
    cleaned = jnp.swapaxes(cleaned.astype(jnp.bfloat16), 1, 2)
    return cleaned, jnp.transpose(ritz, (2, 0, 1))


def from_behind(value, axis, steps):
    count = lax.axis_size(axis)
    pairs = [(source, (source + steps) % count) for source in range(count)]
    return lax.ppermute(value, axis, pairs)


def project_rows(basis_rows, channel_data):
    projected = jnp.einsum(
        "ckr,cmr->ckm", basis_rows, channel_data, precision=lax.Precision.HIGHEST
    )
    return lax.psum(projected, "inp")


def subspace_clean(turned, start_block):
    highest = lax.Precision.HIGHEST
    channel_local, spectra_count, part_count, inputs_width = turned.shape
    row_count = part_count * inputs_width
    channel_data = turned.reshape(channel_local, spectra_count, row_count).astype(jnp.float32)
    start_rows = start_block.reshape(start_block.shape[0], row_count).astype(jnp.float32)
    basis_rows = jnp.broadcast_to(start_rows[None], (channel_local,) + start_rows.shape)
    for iteration in range(ITERS):
        projected = project_rows(basis_rows, channel_data)
        mapped = (
            jnp.einsum("ckm,cmr->ckr", projected, channel_data, precision=highest) / spectra_count
        )
        gram_matrix = jnp.einsum("ckr,cjr->ckj", mapped, mapped, precision=highest)
        gram_matrix = lax.psum(gram_matrix, "inp")
        lower_factor = jnp.linalg.cholesky(gram_matrix)
        basis_rows = lax.linalg.triangular_solve(lower_factor, mapped, left_side=True, lower=True)
    projected = project_rows(basis_rows, channel_data)
    ritz_matrix = (
        jnp.einsum("ckm,cjm->ckj", projected, projected, precision=highest) / spectra_count
    )
    cleaned = channel_data - jnp.einsum("ckm,ckr->cmr", projected, basis_rows, precision=highest)
    cleaned = cleaned.reshape(channel_local, spectra_count, part_count, inputs_width).astype(
        jnp.bfloat16
    )
    return (cleaned, ritz_matrix)


def general_shards(voltages, taps, start):
    slot_count = voltages.shape[0]
    frame_len = voltages.shape[1]
    inputs_local = voltages.shape[2]
    channel_count = frame_len // 2
    tap_count = taps.shape[0]
    frame_stack = voltages.astype(jnp.bfloat16)
    history_len = tap_count - 1
    group_count = lax.axis_size("freq")
    portions = [frame_stack]
    shift_count = (history_len - 1) // slot_count + 1
    for distance in range(1, shift_count + 1):
        first_frame = max(0, distance * slot_count - history_len)
        portion = frame_stack[first_frame:]
        offset_mod = distance % group_count
        arrived = from_behind(portion, "freq", offset_mod)
        portions = [arrived] + portions
    extended = jnp.concatenate(portions, axis=0)
    filtered = jnp.zeros((slot_count, frame_len, inputs_local), jnp.float32)
    for tap_index in range(tap_count):
        window = extended[tap_index : tap_index + slot_count].astype(jnp.float32)
        filtered = filtered + taps[tap_index][None, :, None] * window
    channel_idx = lax.broadcasted_iota(jnp.int32, (channel_count, frame_len), 0)
    sample_idx = lax.broadcasted_iota(jnp.int32, (channel_count, frame_len), 1)
    angles = (channel_idx * sample_idx % frame_len).astype(jnp.float32) * (
        2.0 * math.pi / frame_len
    )
    dft_scale = 1.0 / math.sqrt(channel_count)
    cosine = jnp.cos(angles)
    sine_table = jnp.sin(angles)
    real_part = (
        jnp.einsum("kn,sni->ksi", cosine, filtered, precision=lax.Precision.HIGHEST) * dft_scale
    )
    imag_part = (
        -jnp.einsum("kn,sni->ksi", sine_table, filtered, precision=lax.Precision.HIGHEST)
        * dft_scale
    )
    spectra = jnp.stack([real_part, imag_part], axis=2).astype(jnp.bfloat16)
    turned = lax.all_to_all(spectra, "freq", split_axis=0, concat_axis=1, tiled=True)
    start_local = lax.dynamic_slice_in_dim(
        start, lax.axis_index("inp") * inputs_local, inputs_local, 2
    )
    cleaned, ritz_matrix = subspace_clean(turned, start_local)
    return (cleaned, ritz_matrix)


def start_columns(start, inputs_local):
    return lax.dynamic_slice_in_dim(start, lax.axis_index("inp") * inputs_local, inputs_local, 2)


def shards(voltages, taps, start):
    slots, frame_len, inputs_local = voltages.shape
    count = lax.axis_size("freq")
    fits = (
        count % 2 == 0
        and lax.axis_size("inp") == 4
        and (count * slots + start.shape[0]) % 2 == 0
        and frame_len // 2 == count * LANES
        and inputs_local == CHUNKS * LANES
        and LANES % (count * 16) == 0
        and count * slots <= 32
        and taps.shape[0] <= count * slots
    )
    if not fits:
        return general_shards(voltages, taps, start)
    return clean(channelize(voltages, taps), start_columns(start, inputs_local))


def solution(mesh):
    placed = (P("freq", None, "inp"), P(), P())
    return jax.shard_map(
        shards,
        mesh=mesh,
        in_specs=placed,
        out_specs=(P("freq", None, None, "inp"), P("freq", None, None)),
        check_vma=False,
    )
```

```python
import functools
import math

import jax
import jax.numpy as jnp
import ml_dtypes
import numpy as np
from jax import lax
from jax.experimental import pallas as pl
from jax.experimental.pallas import tpu as pltpu
from jax.sharding import PartitionSpec as P

ITERS = 4
CHUNKS = 2
LANES = 128
MESH = pl.DeviceIdType.MESH


def dft_tables(frame_len, group_count):
    half = frame_len // 2
    pairs = half // 2
    sample = np.arange(half, dtype=np.int64)[:, None]
    tables = []
    for parity in (0, 1):
        channel = 2 * np.arange(pairs, dtype=np.int64)[None, :] + parity
        angle = 2.0 * np.pi * ((sample * channel) % frame_len) / frame_len
        scale = 1.0 / math.sqrt(half)
        real = (np.cos(angle) * scale).reshape(half, group_count, 1, pairs // group_count)
        imag = (-np.sin(angle) * scale).reshape(half, group_count, 1, pairs // group_count)
        table = np.concatenate([real, imag], axis=2).reshape(half, half)
        high = table.astype(ml_dtypes.bfloat16)
        low = (table - high.astype(np.float64)).astype(ml_dtypes.bfloat16)
        tables += [high, low]
    return np.stack(tables)


def channelize_kernel(
    count, slots, tap_count, raw_hbm, taps_ref, table_hbm, spectra_ref,
    raw, volts_ref, gathered, table, halves, outgoing, landed,
    raw_sem, table_sem, send_a, recv_a, send_b, recv_b,
):
    me = lax.axis_index("freq")
    frames = count * slots
    half = table.shape[1]
    rows = volts_ref.shape[3]

    raw_copies = [
        pltpu.make_async_copy(
            raw_hbm.at[:, :, chunk * LANES : (chunk + 1) * LANES], raw.at[chunk], raw_sem.at[chunk]
        )
        for chunk in range(CHUNKS)
    ]
    raw_copies[0].start()
    table_copy = pltpu.make_async_copy(table_hbm, table, table_sem)
    barrier = pltpu.get_barrier_semaphore()
    for step in range(1, count):
        peer = lax.rem(me + step, count)
        pl.semaphore_signal(barrier, inc=1, device_id={"freq": peer}, device_id_type=MESH)

    def turn_input(chunk, frame):
        width = 2 * LANES

        def turn_tile(tile, carry):
            at = pl.ds(pl.multiple_of(tile * width, width), width)
            block = raw[chunk, frame, at, :].astype(jnp.float32).astype(jnp.bfloat16)
            volts_ref[:, chunk, frame, :, at] = block.T.reshape(count, rows, width)
            return carry

        lax.fori_loop(0, 2 * half // width, turn_tile, 0)

    def voltage_copy(chunk, step, frame):
        peer = lax.rem(me + step, count)
        return pltpu.make_async_remote_copy(
            src_ref=volts_ref.at[peer, chunk, frame],
            dst_ref=gathered.at[chunk, me, frame],
            send_sem=send_a.at[chunk, frame, step - 1],
            recv_sem=recv_a.at[chunk, frame, step - 1],
            device_id={"freq": peer},
            device_id_type=MESH,
        )

    def spectra_copy(chunk, step, parity):
        peer = lax.rem(me + step, count)
        return pltpu.make_async_remote_copy(
            src_ref=outgoing.at[peer, chunk, parity],
            dst_ref=landed.at[me, chunk, parity],
            send_sem=send_b.at[chunk, parity, step - 1],
            recv_sem=recv_b.at[chunk, parity, step - 1],
            device_id={"freq": peer},
            device_id_type=MESH,
        )

    order = sorted(range(1, count), key=lambda step: -min(step, count - step))
    raw_copies[0].wait()
    raw_copies[1].start()
    table_copy.start()
    for frame in range(slots):
        turn_input(0, frame)
        if frame == 0:
            pl.semaphore_wait(barrier, count - 1)
        for step in order:
            voltage_copy(0, step, frame).start()
    raw_copies[1].wait()
    for frame in range(slots):
        turn_input(1, frame)
    for chunk in range(CHUNKS):
        gathered[chunk, me] = volts_ref[me, chunk]
    for chunk in range(CHUNKS):
        if chunk == 0:
            for frame in range(slots):
                for step in order:
                    voltage_copy(0, step, frame).wait_send()
                    voltage_copy(1, step, frame).start()
        for frame in range(slots):
            for step in order:
                voltage_copy(chunk, step, frame).wait_recv()

        def filter_tile(tile, carry):
            sums = []
            for part in (0, 1):
                at = pl.ds(pl.multiple_of(tile * LANES + part * half, LANES), LANES)
                window = gathered[chunk, :, :, :, at].astype(jnp.float32)
                window = window.reshape(frames, rows, LANES)
                extended = jnp.concatenate([window[frames - tap_count + 1 :], window], axis=0)
                total = taps_ref[0:1, at][None] * extended[:frames]
                for tap in range(1, tap_count):
                    total = total + taps_ref[tap : tap + 1, at][None] * extended[tap : tap + frames]
                sums.append(total.reshape(frames * rows, LANES))
            at = pl.ds(pl.multiple_of(tile * LANES, LANES), LANES)
            for index, value in ((0, sums[0] + sums[1]), (2, sums[0] - sums[1])):
                high = value.astype(jnp.bfloat16)
                halves[index, :, at] = high
                halves[index + 1, :, at] = (value - high.astype(jnp.float32)).astype(jnp.bfloat16)
            return carry

        lax.fori_loop(0, half // LANES, filter_tile, 0)
        if chunk == 0:
            table_copy.wait()

        def transform_tile(pair, carry):
            at = pl.ds(pl.multiple_of(pair * 2 * LANES, 2 * LANES), 2 * LANES)
            for parity in (0, 1):
                high, low = halves[2 * parity], halves[2 * parity + 1]
                table_high = table[2 * parity, :, at]
                table_low = table[2 * parity + 1, :, at]
                dot = functools.partial(jnp.dot, preferred_element_type=jnp.float32)
                result = dot(low, table_high) + dot(high, table_low) + dot(high, table_high)
                result = result.astype(jnp.bfloat16)
                outgoing[2 * pair, chunk, parity] = result[:, :LANES]
                outgoing[2 * pair + 1, chunk, parity] = result[:, LANES:]
            return carry

        lax.fori_loop(0, count // 2, transform_tile, 0)
        for step in order:
            for frame in range(slots if chunk == 0 else 0):
                voltage_copy(1, step, frame).wait_send()
            spectra_copy(chunk, step, 0).start()
        for step in order:
            spectra_copy(chunk, step, 1).start()
        landed[me, chunk] = outgoing[me, chunk]
    for chunk in range(CHUNKS):
        for parity in (0, 1):
            for step in order:
                spectra_copy(chunk, step, parity).wait()

            def turn_frame(frame, carry):
                at = pl.ds(pl.multiple_of(frame * rows, rows), rows)
                block = landed[:, chunk, parity, at, :].reshape(count * rows, LANES).T
                for part in (0, 1):
                    spectra_ref[
                        parity, part, frame, :, chunk * LANES : (chunk + 1) * LANES
                    ] = block[part * LANES // 2 : (part + 1) * LANES // 2]
                return carry

            lax.fori_loop(0, frames, turn_frame, 0)


def channelize(voltages, taps):
    slots, frame_len, inputs_local = voltages.shape
    count = lax.axis_size("freq")
    half = frame_len // 2
    rows = inputs_local // (count * CHUNKS)
    table = jnp.asarray(dft_tables(frame_len, count))
    all_rows = count * slots * rows
    vmem = pl.BlockSpec(memory_space=pltpu.VMEM)
    spectra = pl.pallas_call(
        functools.partial(channelize_kernel, count, slots, taps.shape[0]),
        out_shape=jax.ShapeDtypeStruct((2, 2, count * slots, LANES // 2, inputs_local), jnp.bfloat16),
        in_specs=[pl.BlockSpec(memory_space=pl.ANY), vmem, pl.BlockSpec(memory_space=pl.ANY)],
        out_specs=vmem,
        scratch_shapes=[
            pltpu.VMEM((CHUNKS, slots, frame_len, LANES), voltages.dtype),
            pltpu.VMEM((count, CHUNKS, slots, rows, frame_len), jnp.bfloat16),
            pltpu.VMEM((CHUNKS, count, slots, rows, frame_len), jnp.bfloat16),
            pltpu.VMEM((4, half, half), jnp.bfloat16),
            pltpu.VMEM((4, all_rows, half), jnp.bfloat16),
            pltpu.VMEM((count, CHUNKS, 2, all_rows, LANES), jnp.bfloat16),
            pltpu.VMEM((count, CHUNKS, 2, all_rows, LANES), jnp.bfloat16),
            pltpu.SemaphoreType.DMA((CHUNKS,)),
            pltpu.SemaphoreType.DMA,
            pltpu.SemaphoreType.DMA((CHUNKS, slots, count - 1)),
            pltpu.SemaphoreType.DMA((CHUNKS, slots, count - 1)),
            pltpu.SemaphoreType.DMA((CHUNKS, 2, count - 1)),
            pltpu.SemaphoreType.DMA((CHUNKS, 2, count - 1)),
        ],
        compiler_params=pltpu.CompilerParams(
            collective_id=0, has_side_effects=True, vmem_limit_bytes=48 * 1024 * 1024
        ),
        name="channelize",
    )(voltages, taps, table)
    spectra = jnp.transpose(spectra, (3, 0, 1, 2, 4))
    return spectra.reshape(LANES, 2, count * slots, inputs_local)


def subspace_kernel(
    own_ref, keep_ref, ritz_ref, gram_ref, from_core, from_chip, send_sem, recv_sem
):
    me = lax.axis_index("inp")
    core = lax.rem(me, 2)
    other_core = me + 1 - 2 * core
    other_chip = lax.rem(me + 2, 4)
    barrier = pltpu.get_barrier_semaphore()
    for peer in (other_core, other_chip):
        pl.semaphore_signal(barrier, inc=1, device_id={"inp": peer}, device_id_type=MESH)
    pl.semaphore_wait(barrier, 2)
    rows = from_core.shape[0]
    mine, other = pl.ds(core * rows, rows), pl.ds((1 - core) * rows, rows)

    def exchange(phase, source, target, peer):
        copy = pltpu.make_async_remote_copy(
            src_ref=source,
            dst_ref=target,
            send_sem=send_sem.at[phase],
            recv_sem=recv_sem.at[phase],
            device_id={"inp": peer},
            device_id_type=MESH,
        )
        copy.start()
        copy.wait()

    exchange(0, own_ref.at[other], from_core, other_core)
    gram_ref[mine] = own_ref[mine] + from_core[...]
    exchange(1, gram_ref.at[mine], from_chip, other_chip)
    gram_ref[mine] = gram_ref[mine] + from_chip[...]
    exchange(2, gram_ref.at[mine], gram_ref.at[mine], other_core)
    block = ritz_ref.shape[0]
    frames = keep_ref.shape[0]

    def times_gram(left):
        total = left[:, 0:1] * gram_ref[block][None]
        for frame in range(1, frames):
            total = total + left[:, frame : frame + 1] * gram_ref[block + frame][None]
        return total

    projected = gram_ref[:block]
    coefficients = None
    for iteration in range(ITERS):
        mapped = projected * (1.0 / frames)
        spread = times_gram(mapped)
        columns = [jnp.sum(spread * mapped[k][None], axis=1) for k in range(block)]
        remaining = [mapped[k] for k in range(block)]
        for k in range(block):
            inverse = lax.rsqrt(columns[k][k : k + 1])
            inverse = inverse * (1.5 - 0.5 * columns[k][k : k + 1] * inverse * inverse)
            factor = columns[k] * inverse
            remaining[k] = remaining[k] * inverse
            for j in range(k + 1, block):
                remaining[j] = remaining[j] - factor[j : j + 1] * remaining[k]
                columns[j] = columns[j] - factor[j : j + 1] * factor
        coefficients = jnp.stack(remaining)
        projected = times_gram(coefficients)
    for k in range(block):
        ritz_ref[k] = jnp.sum(projected * projected[k][None], axis=1) * (1.0 / frames)
    row = lax.broadcasted_iota(jnp.int32, projected.shape[1:], 0)
    for frame in range(frames):
        removed = projected[0][frame : frame + 1] * coefficients[0]
        for k in range(1, block):
            removed = removed + projected[k][frame : frame + 1] * coefficients[k]
        keep_ref[frame] = jnp.where(row == frame, 1.0, 0.0) - removed


def clean(turned, start_local):
    channels, parts, frames, inputs_local = turned.shape
    block = start_local.shape[0]
    begin = jnp.swapaxes(start_local, 0, 1).astype(jnp.bfloat16)
    stacked = jnp.concatenate(
        [jnp.broadcast_to(begin[None], (channels,) + begin.shape), turned], axis=2
    )
    gram = jnp.einsum("cqzi,cqmi->cqzm", stacked, turned, preferred_element_type=jnp.float32)
    gram = jnp.transpose(jnp.sum(gram, axis=1), (1, 2, 0))
    half = ((block + frames) // 2, frames, channels)
    keep, ritz = pl.pallas_call(
        subspace_kernel,
        out_shape=(
            jax.ShapeDtypeStruct((frames, frames, channels), jnp.float32),
            jax.ShapeDtypeStruct((block, block, channels), jnp.float32),
        ),
        scratch_shapes=[
            pltpu.VMEM(gram.shape, jnp.float32),
            pltpu.VMEM(half, jnp.float32),
            pltpu.VMEM(half, jnp.float32),
            pltpu.SemaphoreType.DMA((3,)),
            pltpu.SemaphoreType.DMA((3,)),
        ],
        compiler_params=pltpu.CompilerParams(
            collective_id=1, has_side_effects=True, vmem_limit_bytes=32 * 1024 * 1024
        ),
        name="subspace",
    )(gram)
    keep = jnp.transpose(keep, (2, 0, 1))
    keep = jnp.broadcast_to(keep[:, None], (channels, parts, frames, frames))
    cleaned = jnp.einsum(
        "cqmn,cqni->cqmi", keep, turned.astype(jnp.float32), precision=lax.Precision.HIGHEST
    )
    cleaned = jnp.swapaxes(cleaned.astype(jnp.bfloat16), 1, 2)
    return cleaned, jnp.transpose(ritz, (2, 0, 1))


def from_behind(value, axis, steps):
    count = lax.axis_size(axis)
    pairs = [(source, (source + steps) % count) for source in range(count)]
    return lax.ppermute(value, axis, pairs)


def project_rows(basis_rows, channel_data):
    projected = jnp.einsum(
        "ckr,cmr->ckm", basis_rows, channel_data, precision=lax.Precision.HIGHEST
    )
    return lax.psum(projected, "inp")


def subspace_clean(turned, start_block):
    highest = lax.Precision.HIGHEST
    channel_local, spectra_count, part_count, inputs_width = turned.shape
    row_count = part_count * inputs_width
    channel_data = turned.reshape(channel_local, spectra_count, row_count).astype(jnp.float32)
    start_rows = start_block.reshape(start_block.shape[0], row_count).astype(jnp.float32)
    basis_rows = jnp.broadcast_to(start_rows[None], (channel_local,) + start_rows.shape)
    for iteration in range(ITERS):
        projected = project_rows(basis_rows, channel_data)
        mapped = (
            jnp.einsum("ckm,cmr->ckr", projected, channel_data, precision=highest) / spectra_count
        )
        gram_matrix = jnp.einsum("ckr,cjr->ckj", mapped, mapped, precision=highest)
        gram_matrix = lax.psum(gram_matrix, "inp")
        lower_factor = jnp.linalg.cholesky(gram_matrix)
        basis_rows = lax.linalg.triangular_solve(lower_factor, mapped, left_side=True, lower=True)
    projected = project_rows(basis_rows, channel_data)
    ritz_matrix = (
        jnp.einsum("ckm,cjm->ckj", projected, projected, precision=highest) / spectra_count
    )
    cleaned = channel_data - jnp.einsum("ckm,ckr->cmr", projected, basis_rows, precision=highest)
    cleaned = cleaned.reshape(channel_local, spectra_count, part_count, inputs_width).astype(
        jnp.bfloat16
    )
    return (cleaned, ritz_matrix)


def general_shards(voltages, taps, start):
    slot_count = voltages.shape[0]
    frame_len = voltages.shape[1]
    inputs_local = voltages.shape[2]
    channel_count = frame_len // 2
    tap_count = taps.shape[0]
    frame_stack = voltages.astype(jnp.bfloat16)
    history_len = tap_count - 1
    group_count = lax.axis_size("freq")
    portions = [frame_stack]
    shift_count = (history_len - 1) // slot_count + 1
    for distance in range(1, shift_count + 1):
        first_frame = max(0, distance * slot_count - history_len)
        portion = frame_stack[first_frame:]
        offset_mod = distance % group_count
        arrived = from_behind(portion, "freq", offset_mod)
        portions = [arrived] + portions
    extended = jnp.concatenate(portions, axis=0)
    filtered = jnp.zeros((slot_count, frame_len, inputs_local), jnp.float32)
    for tap_index in range(tap_count):
        window = extended[tap_index : tap_index + slot_count].astype(jnp.float32)
        filtered = filtered + taps[tap_index][None, :, None] * window
    channel_idx = lax.broadcasted_iota(jnp.int32, (channel_count, frame_len), 0)
    sample_idx = lax.broadcasted_iota(jnp.int32, (channel_count, frame_len), 1)
    angles = (channel_idx * sample_idx % frame_len).astype(jnp.float32) * (
        2.0 * math.pi / frame_len
    )
    dft_scale = 1.0 / math.sqrt(channel_count)
    cosine = jnp.cos(angles)
    sine_table = jnp.sin(angles)
    real_part = (
        jnp.einsum("kn,sni->ksi", cosine, filtered, precision=lax.Precision.HIGHEST) * dft_scale
    )
    imag_part = (
        -jnp.einsum("kn,sni->ksi", sine_table, filtered, precision=lax.Precision.HIGHEST)
        * dft_scale
    )
    spectra = jnp.stack([real_part, imag_part], axis=2).astype(jnp.bfloat16)
    turned = lax.all_to_all(spectra, "freq", split_axis=0, concat_axis=1, tiled=True)
    start_local = lax.dynamic_slice_in_dim(
        start, lax.axis_index("inp") * inputs_local, inputs_local, 2
    )
    cleaned, ritz_matrix = subspace_clean(turned, start_local)
    return (cleaned, ritz_matrix)


def start_columns(start, inputs_local):
    return lax.dynamic_slice_in_dim(start, lax.axis_index("inp") * inputs_local, inputs_local, 2)


def shards(voltages, taps, start):
    slots, frame_len, inputs_local = voltages.shape
    count = lax.axis_size("freq")
    fits = (
        count % 2 == 0
        and lax.axis_size("inp") == 4
        and (count * slots + start.shape[0]) % 2 == 0
        and frame_len // 2 == count * LANES
        and inputs_local == CHUNKS * LANES
        and LANES % (count * 16) == 0
        and count * slots <= 32
        and taps.shape[0] <= count * slots
    )
    if not fits:
        return general_shards(voltages, taps, start)
    return clean(channelize(voltages, taps), start_columns(start, inputs_local))


def solution(mesh):
    placed = (P("freq", None, "inp"), P(), P())
    return jax.shard_map(
        shards,
        mesh=mesh,
        in_specs=placed,
        out_specs=(P("freq", None, None, "inp"), P("freq", None, None)),
        check_vma=False,
    )
```
